32 devices in a mesh: segment: 2 (over x), blk: 16 (over z, y, core).
Axes of the slice: x: 2, y: 2, z: 4, core: 2. Of those that a mesh axis runs over, the one named last changes fastest.
Arguments:
- slabs: bfloat16 [32, 2048, 2048], P(None, 'blk'), may hold values from -6 to 6
- orbitals: bfloat16 [2048, 1024], P('blk'), may hold values from -0.125 to 0.125
- channel_orbital: int32 [1024], replicated, may hold values from 0 to 1023
- channel_target: int32 [1024], replicated, may hold values from 0 to 15
- coupling: int32 [16, 16], replicated, may hold values from -16 to 16
Outputs:
- channel_block: bfloat16 [32, 1024, 1024], P(None, 'blk', 'segment')
The draws below stay inside these ranges and needn't reach their ends.
All inputs are finite; a program needn't handle non-finite values.
Results may differ from the reference program's by a relative error of at most 0.0056.
Values may be sent and summed in bfloat16 or wider, within the bound.
No kernel may reach another device: no remote copies, remote signals or barrier semaphores. Data moves between devices by JAX's collectives and lax.ppermute only.
A program may use at most 64 MiB of HBM per device.

```python
import jax
import jax.numpy as jnp
from jax import lax

NB = 2048
NO = 1024
NCH = 1024
NT = 16
SLABS = 32


def plant(entries, key, least, largest):
    extent = entries.shape
    spot = [jax.random.randint(jax.random.fold_in(key, axis), (), 0, extent[axis]) for axis in range(len(extent))]
    entries = entries.at[tuple(spot)].set(least)
    longest = extent.index(max(extent))
    spot[longest] = (spot[longest] + 1) % extent[longest]
    return entries.at[tuple(spot)].set(largest)


def levels(own_key, shape, split, low, high):
    def one(axis_at, parts):
        steps = jax.random.uniform(jax.random.fold_in(jax.random.fold_in(own_key, 6), axis_at), (parts,), jnp.float32, low / len(split), high / len(split))
        return jnp.repeat(jnp.exp(steps), shape[axis_at] // parts).reshape((-1,) + (1,) * (len(shape) - axis_at - 1))

    loudness = one(*split[0])
    for cut in split[1:]:
        loudness = loudness * one(*cut)
    return loudness


def centred(key, shape, spread, bound, split=(), held_as=jnp.bfloat16):
    values = jax.random.normal(key, shape, jnp.float32) * spread
    if len(split) > 0:
        values = levels(key, shape, split, -0.22, 0.18) * values
    return jnp.clip(values, min=-bound, max=bound).astype(held_as)


def setup_inputs(seed: int = 0) -> dict:
    keys = jax.random.split(jax.random.key(seed), 6)
    slabs = centred(keys[0], (SLABS, NB, NB), 1.0, 6.0, ((1, 16),))
    orbitals = centred(keys[1], (NB, NO), NB ** -0.5, 0.125, ((0, 16),))
    channel_orbital = plant(jax.random.randint(keys[2], (NCH,), 0, NO), jax.random.fold_in(keys[2], 1), 0, NO - 1).astype(jnp.int32)
    channel_target = plant(jax.random.randint(keys[3], (NCH,), 0, NT), jax.random.fold_in(keys[3], 1), 0, NT - 1).astype(jnp.int32)
    coupling = plant(jax.random.randint(keys[4], (NT, NT), -16, 17), jax.random.fold_in(keys[4], 1), -16, 16).astype(jnp.int32)
    return {"slabs": slabs, "orbitals": orbitals, "channel_orbital": channel_orbital, "channel_target": channel_target, "coupling": coupling}


def reference(slabs, orbitals, channel_orbital, channel_target, coupling):
    angular = coupling[channel_target][:, channel_target].astype(jnp.float32) / 16.0

    def one_block(slab):
        half = jnp.dot(slab, orbitals, preferred_element_type=jnp.float32).astype(jnp.bfloat16)
        quarter = jnp.dot(orbitals.T, half, preferred_element_type=jnp.float32).astype(jnp.bfloat16)
        picked = quarter[channel_orbital][:, channel_orbital].astype(jnp.float32)
        return (angular * picked).astype(jnp.bfloat16)

    return lax.map(one_block, slabs)
```

```python
import functools

import jax
import jax.numpy as jnp
from jax import lax
from jax.experimental import pallas as pl
from jax.experimental.pallas import tpu as pltpu
from jax.sharding import PartitionSpec as P

CHUNKS = 4
VMEM = 32 * 1024 * 1024


def swap(x, bits):
    n = lax.axis_size("blk")
    return lax.ppermute(x, "blk", [(i, i ^ bits) for i in range(n)])


def params():
    return pltpu.CompilerParams(vmem_limit_bytes=VMEM)


def half_kernel(n, group, where, slab, *refs):
    blocks, outs, panel = refs[:n], refs[n : n + group], refs[n + group]
    step = pl.program_id(0)
    rows = blocks[0].shape[0]

    @pl.when(step == 0)
    def _():
        for v in range(n):
            place = pl.multiple_of((where[group] ^ v) * rows, rows)
            panel[pl.ds(place, rows), :] = blocks[v][...]

    count, depth, width = slab.shape
    result = jnp.dot(
        slab[...].reshape(count * depth, width), panel[...], preferred_element_type=jnp.float32
    )
    result = result.astype(jnp.bfloat16).reshape(outs[0].shape)
    for j in range(group):

        @pl.when(step == j)
        def _(j=j):
            outs[j][...] = result


def first_transform(slabs, blocks, where, group, count):
    n = len(blocks)
    rows, cols = blocks[0].shape
    depth, width = slabs.shape[1:]
    whole = lambda shape: pl.BlockSpec(shape, lambda j, w: (0,) * len(shape))
    return pl.pallas_call(
        functools.partial(half_kernel, n, group),
        out_shape=[jax.ShapeDtypeStruct((count, depth, cols), jnp.bfloat16)] * group,
        grid_spec=pltpu.PrefetchScalarGridSpec(
            num_scalar_prefetch=1,
            grid=(group,),
            in_specs=[pl.BlockSpec((count, depth, width), lambda j, w: (w[j], 0, 0))]
            + [whole((rows, cols))] * n,
            out_specs=[whole((count, depth, cols))] * group,
            scratch_shapes=[pltpu.VMEM((n * rows, cols), jnp.bfloat16)],
        ),
        compiler_params=params(),
        cost_estimate=pl.CostEstimate(
            flops=2 * group * count * depth * width * cols,
            bytes_accessed=2 * group * count * depth * (width + cols) + 2 * n * rows * cols,
            transcendentals=0,
        ),
    )(where, slabs, *blocks)


def quarter_kernel(pieces, side, picked, *refs):
    parts, far, near, panel = refs[:pieces], refs[pieces], refs[pieces + 1], refs[pieces + 2]
    rows = parts[0].shape[1]
    for i in range(pieces):
        panel[i * rows : (i + 1) * rows, :] = parts[i][0]
    share = far.shape[1]
    here = pl.multiple_of(side[0] * share, share)
    there = pl.multiple_of((1 - side[0]) * share, share)
    held = panel[...]
    far[0] = jnp.dot(
        picked[pl.ds(there, share), :], held, preferred_element_type=jnp.float32
    ).astype(jnp.bfloat16)
    near[0] = jnp.dot(picked[pl.ds(here, share), :], held, preferred_element_type=jnp.float32)


def second_transform(picked, parts, side):
    pieces = len(parts)
    count, rows, cols = parts[0].shape
    share = picked.shape[0] // 2
    block = lambda r: pl.BlockSpec((1, r, cols), lambda s, w: (s, 0, 0))
    return pl.pallas_call(
        functools.partial(quarter_kernel, pieces),
        out_shape=[
            jax.ShapeDtypeStruct((count, share, cols), jnp.bfloat16),
            jax.ShapeDtypeStruct((count, share, cols), jnp.float32),
        ],
        grid_spec=pltpu.PrefetchScalarGridSpec(
            num_scalar_prefetch=1,
            grid=(count,),
            in_specs=[pl.BlockSpec(picked.shape, lambda s, w: (0, 0))] + [block(rows)] * pieces,
            out_specs=[block(share), block(share)],
            scratch_shapes=[pltpu.VMEM((pieces * rows, cols), jnp.bfloat16)],
        ),
        compiler_params=params(),
        cost_estimate=pl.CostEstimate(
            flops=4 * count * share * pieces * rows * cols,
            bytes_accessed=2 * count * pieces * rows * cols + 6 * count * share * cols,
            transcendentals=0,
        ),
    )(side, picked, *parts)


def sum_kernel(group, member, near, came, *outs):
    share = outs[0].shape[1]
    for j in range(group):
        rows = pl.ds(pl.multiple_of((member[0] ^ j) * share, share), share)
        total = near[0, rows, :] + came[0, rows, :].astype(jnp.float32)
        outs[j][0] = total.astype(jnp.bfloat16)


def add_sides(near, came, member, group):
    count, rows, cols = near.shape
    block = lambda r: pl.BlockSpec((1, r, cols), lambda s, w: (s, 0, 0))
    return pl.pallas_call(
        functools.partial(sum_kernel, group),
        out_shape=[jax.ShapeDtypeStruct((count, rows // group, cols), jnp.bfloat16)] * group,
        grid_spec=pltpu.PrefetchScalarGridSpec(
            num_scalar_prefetch=1,
            grid=(count,),
            in_specs=[block(rows), block(rows)],
            out_specs=[block(rows // group)] * group,
        ),
        compiler_params=params(),
        cost_estimate=pl.CostEstimate(
            flops=count * rows * cols, bytes_accessed=8 * count * rows * cols, transcendentals=0
        ),
    )(member, near, came)


def on_device(slabs, orbitals, channel_orbital, channel_target, coupling):
    n = lax.axis_size("blk")
    group = n // 4
    segment_now = lax.axis_index("segment")
    me = lax.axis_index("blk")
    core = me % 2
    member = (me // 2) % group
    side = me // (2 * group)
    channels = channel_orbital.shape[0]
    share = channels // n
    half_cols = channels // lax.axis_size("segment")
    slab_count = slabs.shape[0]
    chunks = min(CHUNKS, slab_count // group)
    count = slab_count // (chunks * group)
    splines = jnp.arange(orbitals.shape[1], dtype=jnp.int32)

    picks = lax.dynamic_slice_in_dim(channel_orbital, segment_now * half_cols, half_cols)
    onehot = (splines[:, None] == picks[None, :]).astype(jnp.bfloat16)
    own = jnp.dot(orbitals, onehot, preferred_element_type=jnp.float32).astype(jnp.bfloat16)
    gathered = {0: own}
    bit = n // 2
    while bit:
        gathered.update({v ^ bit: swap(x, bit) for v, x in list(gathered.items())})
        bit //= 2
    column_blocks = [gathered[v] for v in range(n)]

    by_core = channel_orbital.reshape(n // 2, 2, share)

    def pick_rows(kind):
        wanted = lax.dynamic_index_in_dim(by_core, kind, 1, keepdims=False).reshape(-1)
        chosen = (wanted[:, None] == splines[None, :]).astype(jnp.bfloat16)
        return lax.dot_general(
            chosen, orbitals, (((1,), (1,)), ((), ())), preferred_element_type=jnp.float32
        ).astype(jnp.bfloat16)

    pair = jnp.concatenate([pick_rows(core), swap(pick_rows(1 - core), 1)], axis=1)
    pairs = {0: pair}
    bit = group // 2
    while bit:
        pairs.update({j ^ bit: swap(x, 2 * bit) for j, x in list(pairs.items())})
        bit //= 2
    picked = jnp.concatenate([pairs[j] for j in range(group)], axis=1)

    kinds = jnp.arange(coupling.shape[0], dtype=jnp.int32)
    targets_rows = lax.dynamic_slice_in_dim(channel_target, me * share, share)
    targets_cols = lax.dynamic_slice_in_dim(channel_target, segment_now * half_cols, half_cols)
    onehot_rows = (targets_rows[:, None] == kinds[None, :]).astype(jnp.float32)
    onehot_cols = (kinds[:, None] == targets_cols[None, :]).astype(jnp.float32)
    angular = (
        jnp.dot(
            jnp.dot(
                onehot_rows, coupling.astype(jnp.float32), precision=lax.Precision.HIGHEST
            ),
            onehot_cols,
            precision=lax.Precision.HIGHEST,
        )
        / 16.0
    )

    order = member ^ jnp.arange(group, dtype=jnp.int32)
    out = jnp.zeros((slab_count, share, half_cols), jnp.bfloat16)
    for k in range(chunks):
        where = jnp.concatenate([k * group + order, me[None]])
        halves = first_transform(slabs, column_blocks, where, group, count)
        came = [halves[0]] + [swap(halves[j], 2 * j) for j in range(1, group)]
        parts = []
        for x in came:
            parts += [x, swap(x, 1)]
        far, near = second_transform(picked, parts, side[None])
        quarters = add_sides(near, swap(far, n // 2), member[None], group)
        for j in range(group):
            mine = quarters[j] if j == 0 else swap(quarters[j], 2 * j)
            value = (angular[None] * mine.astype(jnp.float32)).astype(jnp.bfloat16)
            first = (k * group + (member ^ j)) * count
            out = lax.dynamic_update_slice(out, value, (first, 0, 0))
    return out


def solution(mesh):
    return jax.shard_map(
        on_device,
        mesh=mesh,
        in_specs=(P(None, "blk", None), P("blk", None), P(), P(), P()),
        out_specs=P(None, "blk", "segment"),
        check_vma=False,
    )
```

```python
import jax
import jax.numpy as jnp
from jax import lax
from jax.experimental import pallas as pl
from jax.experimental.pallas import tpu as pltpu
from jax.sharding import PartitionSpec as P

VMEM = 49 * 1024 * 1024


def swap(x, bits):
    n = lax.axis_size("blk")
    return lax.ppermute(x, "blk", [(i, i ^ bits) for i in range(n)])


def plan(total):
    if total < 4:
        return [1] * total
    inner = total - 2
    return [1] + [2] * (inner // 2) + [1] * (inner % 2) + [1]


class Step:
    def __init__(self, body, outs, ins, scratch=(), aliases=None):
        self.body, self.outs, self.ins = body, outs, ins
        self.scratch, self.aliases = list(scratch), aliases or {}


def call(steps, tokens=()):
    ins = [x for step in steps for x in step.ins]
    outs = [x for step in steps for x in step.outs]
    scratch = [x for step in steps for x in step.scratch]
    aliases, first_in, first_out = {}, 0, 0
    for step in steps:
        aliases.update({first_in + i: first_out + o for i, o in step.aliases.items()})
        first_in += len(step.ins)
        first_out += len(step.outs)

    def body(*refs):
        left = [list(refs[: len(ins)]), list(refs[len(ins) + len(tokens) :])]
        left = [left[0], left[1][: len(outs)], left[1][len(outs) :]]

        def take(which, amount):
            taken, left[which] = left[which][:amount], left[which][amount:]
            return taken

        running = [
            step.body(
                take(0, len(step.ins)), take(1, len(step.outs)), take(2, len(step.scratch))
            )
            for step in steps
        ]
        for _ in range(3):
            for each in running:
                next(each, None)

    results = pl.pallas_call(
        body,
        out_shape=[jax.ShapeDtypeStruct(shape, kind) for shape, kind, _ in outs],
        in_specs=[pl.BlockSpec(memory_space=space) for _, space in ins]
        + [pl.BlockSpec(memory_space=pl.ANY)] * len(tokens),
        out_specs=[pl.BlockSpec(memory_space=space) for _, _, space in outs],
        scratch_shapes=scratch,
        input_output_aliases=aliases,
        compiler_params=pltpu.CompilerParams(vmem_limit_bytes=VMEM),
        cost_estimate=pl.CostEstimate(flops=0, bytes_accessed=0, transcendentals=0),
    )(*[x for x, _ in ins], *tokens)
    results = list(results)
    split = []
    for step in steps:
        split.append(results[: len(step.outs)])
        results = results[len(step.outs) :]
    return split


def inside(xs):
    return [(x, pltpu.VMEM) for x in xs]


def scalar(x):
    return [(x.reshape(-1).astype(jnp.int32), pltpu.SMEM)]


def after(xs, tokens):
    def body(ins, outs, scratch):
        yield

    outs = [(x.shape, x.dtype, pl.ANY) for x in xs]
    ins = [(x, pl.ANY) for x in xs]
    return call([Step(body, outs, ins, aliases={i: i for i in range(len(xs))})], tokens)[0]


def first_transform(slabs, blocks, where, group, count):
    n = len(blocks)
    rows, cols = blocks[0].shape
    depth, width = slabs.shape[1:]

    def body(ins, outs, scratch):
        place, slab_hbm, *held = ins
        panel, buffer, sems = scratch
        copies = []
        for j in range(group):
            source = slab_hbm.at[pl.ds(place[j], count)]
            copies.append(pltpu.make_async_copy(source, buffer.at[j], sems.at[j]))
            copies[j].start()
        yield
        for v in range(n):
            first = pl.multiple_of((place[group] ^ v) * rows, rows)
            panel[pl.ds(first, rows), :] = held[v][...]
        for j in range(group):
            copies[j].wait()
            result = jnp.dot(
                buffer[j].reshape(count * depth, width),
                panel[...],
                preferred_element_type=jnp.float32,
            )
            outs[j][...] = result.astype(jnp.bfloat16).reshape(count, depth, cols)

    return Step(
        body,
        [((count, depth, cols), jnp.bfloat16, pltpu.VMEM)] * group,
        scalar(where) + [(slabs, pltpu.HBM)] + inside(blocks),
        [
            pltpu.VMEM((n * rows, cols), jnp.bfloat16),
            pltpu.VMEM((group, count, depth, width), jnp.bfloat16),
            pltpu.SemaphoreType.DMA((group,)),
        ],
    )


def second_transform(picked, parts, side):
    pieces = len(parts)
    count, rows, cols = parts[0].shape
    share = picked.shape[0] // 2

    def body(ins, outs, scratch):
        side_now, picked_ref, *held = ins
        far, near = outs
        panel = scratch[0]
        yield
        here = pl.multiple_of(side_now[0] * share, share)
        there = pl.multiple_of((1 - side_now[0]) * share, share)
        for s in range(count):
            for i in range(pieces):
                panel[s, i * rows : (i + 1) * rows, :] = held[i][s]
        for s in range(count):
            far[s] = jnp.dot(
                picked_ref[pl.ds(there, share), :], panel[s], preferred_element_type=jnp.float32
            ).astype(jnp.bfloat16)
            near[s] = jnp.dot(
                picked_ref[pl.ds(here, share), :], panel[s], preferred_element_type=jnp.float32
            )

    return Step(
        body,
        [
            ((count, share, cols), jnp.bfloat16, pltpu.VMEM),
            ((count, share, cols), jnp.float32, pltpu.VMEM),
        ],
        scalar(side) + inside([picked]) + inside(parts),
        [pltpu.VMEM((count, pieces * rows, cols), jnp.bfloat16)],
    )


def add_sides(near, came, member, group):
    count, rows, cols = near.shape
    share = rows // group

    def body(ins, outs, scratch):
        member_now, near_ref, came_ref = ins
        yield
        for j in range(group):
            mine = pl.ds(pl.multiple_of((member_now[0] ^ j) * share, share), share)
            for s in range(count):
                total = near_ref[s, mine, :] + came_ref[s, mine, :].astype(jnp.float32)
                outs[j][s] = total.astype(jnp.bfloat16)

    return Step(
        body,
        [((count, share, cols), jnp.bfloat16, pltpu.VMEM)] * group,
        scalar(member) + inside([near, came]),
    )


def scale_into(out, angular, mine, place):
    group = len(mine)
    count, share, cols = mine[0].shape

    def body(ins, outs, scratch):
        place_now, angular_ref, *held = ins[:-1]
        buffer, sems = scratch
        yield
        copies = []
        for j in range(group):
            for s in range(count):
                value = angular_ref[...] * held[j][s].astype(jnp.float32)
                buffer[j, s] = value.astype(jnp.bfloat16)
            target = outs[0].at[pl.ds(place_now[j], count)]
            copies.append(pltpu.make_async_copy(buffer.at[j], target, sems.at[j]))
            copies[j].start()
        yield
        for copy in copies:
            copy.wait()

    return Step(
        body,
        [(out.shape, out.dtype, pltpu.HBM)],
        scalar(place) + inside([angular]) + inside(mine) + [(out, pltpu.HBM)],
        [
            pltpu.VMEM((group, count, share, cols), jnp.bfloat16),
            pltpu.SemaphoreType.DMA((group,)),
        ],
        {2 + group: 0},
    )


def on_device(slabs, orbitals, channel_orbital, channel_target, coupling):
    n = lax.axis_size("blk")
    group = n // 4
    segment_now = lax.axis_index("segment")
    me = lax.axis_index("blk")
    core = me % 2
    member = (me // 2) % group
    side = me // (2 * group)
    channels = channel_orbital.shape[0]
    share = channels // n
    half_cols = channels // lax.axis_size("segment")
    slab_count = slabs.shape[0]
    splines = jnp.arange(orbitals.shape[1], dtype=jnp.int32)

    picks = lax.dynamic_slice_in_dim(channel_orbital, segment_now * half_cols, half_cols)
    onehot = (splines[:, None] == picks[None, :]).astype(jnp.bfloat16)
    own = jnp.dot(orbitals, onehot, preferred_element_type=jnp.float32).astype(jnp.bfloat16)
    gathered = {0: own}
    bit = n // 2
    while bit:
        gathered.update({v ^ bit: swap(x, bit) for v, x in list(gathered.items())})
        bit //= 2
    column_blocks = [gathered[v] for v in range(n)]

    by_core = channel_orbital.reshape(n // 2, 2, share)

    def pick_rows(kind):
        wanted = lax.dynamic_index_in_dim(by_core, kind, 1, keepdims=False).reshape(-1)
        chosen = (wanted[:, None] == splines[None, :]).astype(jnp.bfloat16)
        return lax.dot_general(
            chosen, orbitals, (((1,), (1,)), ((), ())), preferred_element_type=jnp.float32
        ).astype(jnp.bfloat16)

    pair = jnp.concatenate([pick_rows(core), swap(pick_rows(1 - core), 1)], axis=1)

    def all_rows(pair):
        pairs = {0: pair}
        bit = group // 2
        while bit:
            pairs.update({j ^ bit: swap(x, 2 * bit) for j, x in list(pairs.items())})
            bit //= 2
        return jnp.concatenate([pairs[j] for j in range(group)], axis=1)

    kinds = jnp.arange(coupling.shape[0], dtype=jnp.int32)
    targets_rows = lax.dynamic_slice_in_dim(channel_target, me * share, share)
    targets_cols = lax.dynamic_slice_in_dim(channel_target, segment_now * half_cols, half_cols)
    onehot_rows = (targets_rows[:, None] == kinds[None, :]).astype(jnp.float32)
    onehot_cols = (kinds[:, None] == targets_cols[None, :]).astype(jnp.float32)
    angular = (
        jnp.dot(
            jnp.dot(
                onehot_rows, coupling.astype(jnp.float32), precision=lax.Precision.HIGHEST
            ),
            onehot_cols,
            precision=lax.Precision.HIGHEST,
        )
        / 16.0
    )

    order = member ^ jnp.arange(group, dtype=jnp.int32)
    counts = plan(slab_count // group)
    starts = [sum(counts[:k]) * group for k in range(len(counts))]

    def halves_of(k):
        where = jnp.concatenate([starts[k] + order * counts[k], me[None]])
        return first_transform(slabs, column_blocks, where, group, counts[k])

    def send(halves):
        return [halves[0]] + [swap(halves[j], 2 * j) for j in range(1, group)]

    out = jnp.zeros((slab_count, share, half_cols), jnp.bfloat16)
    last = len(counts) - 1
    halves, came, near, across, quarters = {}, {}, {}, {}, {}
    halves[0] = call([halves_of(0)])[0]
    came[0] = send(halves[0])
    token = halves[0][0]
    for k in range(1, min(3, last + 1)):
        halves[k] = call([halves_of(k)], [token])[0]
        token = halves[k][0]
    picked = all_rows(after([pair], [halves[0][0]])[0])

    for k in range(last + 4):
        steps, names = [], []
        if k <= last:
            held = after(came[k] + (halves[k + 1] if k < last else []), [token])
            came[k] = held[:group]
            parts = []
            for x in came[k]:
                parts += [x, swap(x, 1)]
            if k < last:
                came[k + 1] = send(held[group:])
            steps.append(second_transform(picked, parts, side))
            names.append("second")
        if 0 <= k - 2 <= last:
            steps.append(add_sides(near[k - 2], across[k - 2], member, group))
            names.append("add")
        if 0 <= k - 3 <= last:
            j = k - 3
            mine = [quarters[j][0]] + [swap(quarters[j][i], 2 * i) for i in range(1, group)]
            steps.append(scale_into(out, angular, mine, starts[j] + order * counts[j]))
            names.append("scale")
        if k + 3 <= last:
            steps.append(halves_of(k + 3))
            names.append("first")
        for name, result in zip(names, call(steps), strict=True):
            if name == "second":
                far, near[k] = result
                across[k] = swap(far, n // 2)
            elif name == "add":
                quarters[k - 2] = result
            elif name == "scale":
                out = result[0]
            else:
                halves[k + 3] = result
            token = result[0]
    return out


def solution(mesh):
    return jax.shard_map(
        on_device,
        mesh=mesh,
        in_specs=(P(None, "blk", None), P("blk", None), P(), P(), P()),
        out_specs=P(None, "blk", "segment"),
        check_vma=False,
    )
```

```python
import jax
import jax.numpy as jnp
from jax import lax
from jax.experimental import pallas as pl
from jax.experimental.pallas import tpu as pltpu
from jax.sharding import PartitionSpec as P

MIB = 1024 * 1024
LONG = 10**11


def swap(x, bits):
    n = lax.axis_size("blk")
    return lax.ppermute(x, "blk", [(i, i ^ bits) for i in range(n)])


class Step:
    def __init__(self, body, outs, ins, scratch=(), aliases=None, work=0):
        self.body, self.outs, self.ins, self.work = body, outs, ins, work
        self.scratch, self.aliases = list(scratch), aliases or {}


def call(steps, tokens=(), room=20):
    ins = [x for step in steps for x in step.ins]
    outs = [x for step in steps for x in step.outs]
    scratch = [x for step in steps for x in step.scratch]
    aliases, first_in, first_out = {}, 0, 0
    for step in steps:
        aliases.update({first_in + i: first_out + o for i, o in step.aliases.items()})
        first_in += len(step.ins)
        first_out += len(step.outs)

    def body(*refs):
        left = [list(refs[: len(ins)]), list(refs[len(ins) + len(tokens) :])]
        left = [left[0], left[1][: len(outs)], left[1][len(outs) :]]

        def take(which, amount):
            taken, left[which] = left[which][:amount], left[which][amount:]
            return taken

        running = [
            step.body(
                take(0, len(step.ins)), take(1, len(step.outs)), take(2, len(step.scratch))
            )
            for step in steps
        ]
        for _ in range(3):
            for each in running:
                next(each, None)

    results = pl.pallas_call(
        body,
        out_shape=[jax.ShapeDtypeStruct(shape, kind) for shape, kind, _ in outs],
        in_specs=[pl.BlockSpec(memory_space=space) for _, space in ins]
        + [pl.BlockSpec(memory_space=pl.ANY)] * len(tokens),
        out_specs=[pl.BlockSpec(memory_space=space) for _, _, space in outs],
        scratch_shapes=scratch,
        input_output_aliases=aliases,
        compiler_params=pltpu.CompilerParams(vmem_limit_bytes=room * MIB),
        cost_estimate=pl.CostEstimate(
            flops=sum(step.work for step in steps), bytes_accessed=0, transcendentals=0
        ),
    )(*[x for x, _ in ins], *tokens)
    results = list(results)
    split = []
    for step in steps:
        split.append(results[: len(step.outs)])
        results = results[len(step.outs) :]
    return split


def inside(xs):
    return [(x, pltpu.VMEM) for x in xs]


def outside(xs):
    return [(x, pl.ANY) for x in xs]


def scalar(x):
    return [(x.reshape(-1).astype(jnp.int32), pltpu.SMEM)]


def plan(slab_count, group):
    full = slab_count // (2 * group)
    return [1] if full < 2 else [2] + [1] * (full - 1) + [2]


def after(xs, tokens, work=0):
    def body(ins, outs, scratch):
        yield

    outs = [(x.shape, x.dtype, pl.ANY) for x in xs]
    step = Step(body, outs, outside(xs), aliases={i: i for i in range(len(xs))}, work=work)
    return call([step], tokens)[0]


def first_transform(slabs, blocks, me, core, firsts, cuts, group, work=0):
    n = len(blocks)
    rows, cols = blocks[0].shape
    depth, width = slabs.shape[1:]
    amounts = [group if cut == 2 else 2 * group for cut in cuts]
    begins = [sum(amounts[:i]) for i in range(len(cuts))]

    def body(ins, outs, scratch):
        me_now, core_now, place, slab_hbm, *held = ins
        panel, buffer, sems = scratch
        copies = [
            [
                pltpu.make_async_copy(
                    slab_hbm.at[place[begins[i] + j]], buffer.at[i % 2, j], sems.at[i % 2, j]
                )
                for j in range(amount)
            ]
            for i, amount in enumerate(amounts)
        ]
        for batch in copies[:2]:
            for copy in batch:
                copy.start()
        yield
        for v in range(n):
            first = pl.multiple_of((me_now[0] ^ v) * rows, rows)
            panel[pl.ds(first, rows), :] = held[v][...]
        for i, amount in enumerate(amounts):
            for copy in copies[i]:
                copy.wait()
            result = jnp.dot(
                buffer[i % 2, :amount].reshape(amount * depth, width),
                panel[...],
                preferred_element_type=jnp.float32,
            )
            result = result.astype(jnp.bfloat16).reshape(amount, depth, cols)
            kept, other = outs[2 * i : 2 * i + 2]
            if cuts[i] == 1:
                kept[...], other[...] = result[:group], result[group:]
            else:
                low, high = result[:, :, : cols // 2], result[:, :, cols // 2 :]

                @pl.when(core_now[0] == 0)
                def _(kept=kept, other=other, low=low, high=high):
                    kept[...], other[...] = low, high

                @pl.when(core_now[0] == 1)
                def _(kept=kept, other=other, low=low, high=high):
                    kept[...], other[...] = high, low

            for batch in copies[i + 2 : i + 3]:
                for copy in batch:
                    copy.start()

    return Step(
        body,
        [
            ((group, depth, cols // cut), jnp.bfloat16, pltpu.VMEM)
            for cut in cuts
            for _ in range(2)
        ],
        scalar(me) + scalar(core) + scalar(firsts) + [(slabs, pltpu.HBM)] + inside(blocks),
        [
            pltpu.VMEM((n * rows, cols), jnp.bfloat16),
            pltpu.VMEM((2, max(amounts), depth, width), jnp.bfloat16),
            pltpu.SemaphoreType.DMA((2, max(amounts))),
        ],
        work=work,
    )


def merge_cores(kept, came):
    group, depth, cols = kept.shape

    def body(ins, outs, scratch):
        yield
        for j in range(group):
            outs[j][:depth, :] = ins[0][j]
            outs[j][depth:, :] = ins[1][j]

    return Step(
        body, [((2 * depth, cols), jnp.bfloat16, pltpu.VMEM)] * group, inside([kept, came])
    )


def pick_rows(chosen, blocks, work):
    rows, width = blocks[0].shape
    listed = chosen.shape[0]
    amount = len(blocks)

    def body(ins, outs, scratch):
        chosen_ref, *held = ins
        buffer, sems = scratch
        copies = []
        for i in range(amount):
            target = buffer.at[pl.ds(i * rows, rows)]
            copies.append(pltpu.make_async_copy(held[i], target, sems.at[i]))
            copies[i].start()
        yield
        for i in range(0, amount, 2):
            copies[i].wait()
            copies[i + 1].wait()
            result = lax.dot_general(
                chosen_ref[...],
                buffer[i * rows : (i + 2) * rows, :],
                (((1,), (1,)), ((), ())),
                preferred_element_type=jnp.float32,
            )
            outs[0][:, i * rows : (i + 2) * rows] = result.astype(jnp.bfloat16)

    return Step(
        body,
        [((listed, rows * amount), jnp.bfloat16, pltpu.VMEM)],
        inside([chosen]) + outside(blocks),
        [
            pltpu.VMEM((rows * amount, width), jnp.bfloat16),
            pltpu.SemaphoreType.DMA((amount,)),
        ],
        work=work,
    )


def second_transform(picked, parts, side, work):
    rows, cols = parts[0].shape
    share = picked.shape[0] // 2

    def body(ins, outs, scratch):
        side_now, picked_ref, *held = ins
        far, near = outs
        yield
        here = pl.ds(pl.multiple_of(side_now[0] * share, share), share)
        there = pl.ds(pl.multiple_of((1 - side_now[0]) * share, share), share)

        def total(lines):
            return sum(
                jnp.dot(
                    picked_ref[lines, j * rows : (j + 1) * rows],
                    x[...],
                    preferred_element_type=jnp.float32,
                )
                for j, x in enumerate(held)
            )

        far[...] = total(there).astype(jnp.bfloat16)
        near[...] = total(here)

    return Step(
        body,
        [
            ((share, cols), jnp.bfloat16, pltpu.VMEM),
            ((share, cols), jnp.float32, pltpu.VMEM),
        ],
        scalar(side) + inside([picked] + parts),
        work=work,
    )


def add_sides(near, came, member, group, work):
    rows, cols = near.shape
    share = rows // group

    def body(ins, outs, scratch):
        member_now, near_ref, came_ref = ins
        yield
        for j in range(group):
            lines = pl.ds(pl.multiple_of((member_now[0] ^ j) * share, share), share)
            total = near_ref[lines, :] + came_ref[lines, :].astype(jnp.float32)
            outs[j][...] = total.astype(jnp.bfloat16)

    return Step(
        body,
        [((share, cols), jnp.bfloat16, pltpu.VMEM)] * group,
        scalar(member) + inside([near, came]),
        work=work,
    )


def for_other_core(held, core):
    group = len(held)
    share, cols = held[0].shape[0] // 2, held[0].shape[1]

    def body(ins, outs, scratch):
        core_now, *refs = ins
        yield
        lines = pl.ds(pl.multiple_of((1 - core_now[0]) * share, share), share)
        for j, x in enumerate(refs):
            outs[0][j] = x[lines, :]

    return Step(
        body,
        [((group, share, cols), jnp.bfloat16, pltpu.VMEM)],
        scalar(core) + inside(held),
    )


def scale(slab_count, angular, held, came, order, core, cuts):
    share, cols = angular.shape
    group = len(held[0])
    chunks = len(cuts)

    def body(ins, outs, scratch):
        place, core_now, angular_ref, *refs = ins
        mine, theirs, sems = scratch
        lines = pl.ds(pl.multiple_of(core_now[0] * share, share), share)
        copies = []
        for k, cut in enumerate(cuts):
            wide = pl.ds(0, cols // cut)
            pairs = [(refs[k * group + j].at[lines], mine.at[k, j, :, wide]) for j in range(group)]
            pairs.append((refs[chunks * group + k], theirs.at[k, :, :, wide]))
            for source, target in pairs:
                copies.append(pltpu.make_async_copy(source, target, sems.at[len(copies)]))
                copies[-1].start()
        yield
        first = 0
        for k, cut in enumerate(cuts):
            for copy in copies[k * (group + 1) : (k + 1) * (group + 1)]:
                copy.wait()
            for kind in range(2):
                source = core_now[0] if kind == 0 else 1 - core_now[0]
                lanes = slice(None)
                if cut == 2:
                    lanes = pl.ds(pl.multiple_of(source * (cols // 2), cols // 2), cols // 2)
                factor = angular_ref[:, lanes]
                for j in range(group):
                    slab = first + place[j] * (3 - cut) + (source if cut == 1 else 0)
                    x = (mine if kind == 0 else theirs)[k, j, :, : cols // cut]
                    value = factor * x.astype(jnp.float32)
                    outs[0][slab, :, lanes] = value.astype(jnp.bfloat16)
            first += group * (3 - cut)

    flat = [x for xs in held for x in xs]
    return Step(
        body,
        [((slab_count, share, cols), jnp.bfloat16, pltpu.VMEM)],
        scalar(order) + scalar(core) + inside([angular]) + outside(flat + came),
        [
            pltpu.VMEM((chunks, group, share, cols), jnp.bfloat16),
            pltpu.VMEM((chunks, group, share, cols), jnp.bfloat16),
            pltpu.SemaphoreType.DMA((chunks * (group + 1),)),
        ],
    )


def on_device(slabs, orbitals, channel_orbital, channel_target, coupling):
    n = lax.axis_size("blk")
    group = n // 4
    segment_now = lax.axis_index("segment")
    me = lax.axis_index("blk")
    core = me % 2
    member = (me // 2) % group
    side = me // (2 * group)
    channels = channel_orbital.shape[0]
    share = channels // n
    half_cols = channels // lax.axis_size("segment")
    slab_count = slabs.shape[0]
    splines = jnp.arange(orbitals.shape[1], dtype=jnp.int32)

    picks = lax.dynamic_slice_in_dim(channel_orbital, segment_now * half_cols, half_cols)
    onehot = (splines[:, None] == picks[None, :]).astype(jnp.bfloat16)
    mine = jnp.dot(orbitals, onehot, preferred_element_type=jnp.float32).astype(jnp.bfloat16)
    gathered = {0: mine}
    rows_of = {0: orbitals}
    bit = n // 2
    while bit:
        for v, x in list(gathered.items()):
            gathered[v ^ bit] = swap(x, bit)
        if bit == n // 2:
            rows_of[n // 4] = swap(orbitals, n // 4)
            gathered[bit] = after([gathered[bit]], [rows_of[n // 4]])[0]
        bit //= 2
    column_blocks = [gathered[v] for v in range(n)]

    kinds = jnp.arange(coupling.shape[0], dtype=jnp.int32)
    targets_rows = lax.dynamic_slice_in_dim(channel_target, me * share, share)
    targets_cols = lax.dynamic_slice_in_dim(channel_target, segment_now * half_cols, half_cols)
    onehot_rows = (targets_rows[:, None] == kinds[None, :]).astype(jnp.float32)
    onehot_cols = (kinds[:, None] == targets_cols[None, :]).astype(jnp.float32)
    angular = (
        jnp.dot(
            jnp.dot(
                onehot_rows, coupling.astype(jnp.float32), precision=lax.Precision.HIGHEST
            ),
            onehot_cols,
            precision=lax.Precision.HIGHEST,
        )
        / 16.0
    )

    order = member ^ jnp.arange(group, dtype=jnp.int32)
    cuts = plan(slab_count, group)
    last = len(cuts) - 1
    starts = [sum(group * (3 - cut) for cut in cuts[:k]) for k in range(last + 1)]
    kept, other, own, came, near, across, sums, held = {}, {}, {}, {}, {}, {}, {}, {}

    def transform(ks, tokens, work=0, trade=True):
        firsts = []
        for k in ks:
            if cuts[k] == 2:
                firsts.append(starts[k] + order)
            else:
                firsts += [starts[k] + 2 * order + core, starts[k] + 2 * order + 1 - core]
        step = first_transform(
            slabs,
            column_blocks,
            me,
            core,
            jnp.concatenate(firsts),
            [cuts[k] for k in ks],
            group,
            work,
        )
        flat = call([step], tokens, 46)[0]
        for i, k in enumerate(ks):
            kept[k], other[k] = flat[2 * i : 2 * i + 2]
            if trade:
                other[k] = swap(other[k], 1)

    def merge(ks, tokens):
        steps = [merge_cores(kept[k], other[k]) for k in ks]
        for k, result in zip(ks, call(steps, tokens), strict=True):
            own[k] = result

    def send(xs):
        return [swap(xs[j], 2 * j) for j in range(1, group)]

    transform([0], [angular])
    merge([0], [])
    came[0] = send(own[0])
    bit = group // 2
    while bit > 1:
        for v, x in list(rows_of.items()):
            rows_of[v ^ bit] = swap(x, bit)
        bit //= 2
    clock = after([jnp.zeros((8, 128), jnp.float32)], [own[0][0]], LONG)[0]
    if last:
        transform(list(range(1, last + 1)), [clock], 0, False)
        clock = kept[last]
    arrived = [v for v in rows_of if v]
    ready = after(
        came[0] + [rows_of[v] for v in arrived] + [other[k] for k in range(1, last + 1)], [clock]
    )
    came[0], ready = ready[: group - 1], ready[group - 1 :]
    rows_of.update(zip(arrived, ready, strict=False))
    for k in range(1, last + 1):
        other[k] = swap(ready[len(arrived) + k - 1], 1)
    token = came[0][0]
    if last:
        merge([1], [token])
        came[1] = send(own[1])
    for v, x in list(rows_of.items()):
        rows_of[v ^ 1] = swap(x, 1)

    chosen = (channel_orbital[:, None] == splines[None, :]).astype(jnp.bfloat16)
    rows = [rows_of[2 * j + c] for j in range(group) for c in range(2)]
    picked = call([pick_rows(chosen, rows, LONG)], [token])[0][0]

    token = picked
    for k in range(last + 1):
        step = second_transform(picked, [own[k][0]] + came[k], side, LONG if k else 0)
        far, near[k] = call([step], [token])[0]
        across[k] = swap(far, n // 2)
        token = far
        if k == 0 and last > 1:
            merge(list(range(2, last + 1)), [token])
        if 0 < k < last:
            came[k + 1] = send([None] + after(own[k + 1][1:], [before]))
        before = far
        if k:
            late = held[k - 2][1:] if k > 1 else []
            sums[k - 1] = call(
                [add_sides(near[k - 1], across[k - 1], member, group, LONG)], [token] + late
            )[0]
            held[k - 1] = [sums[k - 1][0]] + send(sums[k - 1])
            token = sums[k - 1][0]
    clock = token
    final = {}
    for k in range(last):
        final[k] = swap(call([for_other_core(held[k], core)], [token])[0][0], 1)
    sums[last] = call([add_sides(near[last], across[last], member, group, 0)], [clock])[0]
    held[last] = [sums[last][0]] + send(sums[last])
    final[last] = swap(call([for_other_core(held[last], core)])[0][0], 1)
    ks = range(last + 1)
    step = scale(
        slab_count, angular, [held[k] for k in ks], [final[k] for k in ks], order, core, cuts
    )
    return call([step], (), 40)[0][0]


def solution(mesh):
    return jax.shard_map(
        on_device,
        mesh=mesh,
        in_specs=(P(None, "blk", None), P("blk", None), P(), P(), P()),
        out_specs=P(None, "blk", "segment"),
        check_vma=False,
    )
```

```python
import jax
import jax.numpy as jnp
from jax import lax
from jax.experimental import pallas as pl
from jax.experimental.pallas import tpu as pltpu
from jax.sharding import PartitionSpec as P

MIB = 1024 * 1024
MIDDLE = 3 * 10**9
LONG = 10**11


def swap(x, bits):
    n = lax.axis_size("blk")
    return lax.ppermute(x, "blk", [(i, i ^ bits) for i in range(n)])


class Step:
    def __init__(self, body, outs, ins, scratch=(), aliases=None, work=0):
        self.body, self.outs, self.ins, self.work = body, outs, ins, work
        self.scratch, self.aliases = list(scratch), aliases or {}


def call(steps, tokens=(), room=20):
    ins = [x for step in steps for x in step.ins]
    outs = [x for step in steps for x in step.outs]
    scratch = [x for step in steps for x in step.scratch]
    aliases, first_in, first_out = {}, 0, 0
    for step in steps:
        aliases.update({first_in + i: first_out + o for i, o in step.aliases.items()})
        first_in += len(step.ins)
        first_out += len(step.outs)

    def body(*refs):
        left = [list(refs[: len(ins)]), list(refs[len(ins) + len(tokens) :])]
        left = [left[0], left[1][: len(outs)], left[1][len(outs) :]]

        def take(which, amount):
            taken, left[which] = left[which][:amount], left[which][amount:]
            return taken

        running = [
            step.body(
                take(0, len(step.ins)), take(1, len(step.outs)), take(2, len(step.scratch))
            )
            for step in steps
        ]
        for _ in range(3):
            for each in running:
                next(each, None)

    results = pl.pallas_call(
        body,
        out_shape=[jax.ShapeDtypeStruct(shape, kind) for shape, kind, _ in outs],
        in_specs=[pl.BlockSpec(memory_space=space) for _, space in ins]
        + [pl.BlockSpec(memory_space=pl.ANY)] * len(tokens),
        out_specs=[pl.BlockSpec(memory_space=space) for _, _, space in outs],
        scratch_shapes=scratch,
        input_output_aliases=aliases,
        compiler_params=pltpu.CompilerParams(vmem_limit_bytes=room * MIB),
        cost_estimate=pl.CostEstimate(
            flops=sum(step.work for step in steps), bytes_accessed=0, transcendentals=0
        ),
    )(*[x for x, _ in ins], *tokens)
    results = list(results)
    split = []
    for step in steps:
        split.append(results[: len(step.outs)])
        results = results[len(step.outs) :]
    return split


def inside(xs):
    return [(x, pltpu.VMEM) for x in xs]


def outside(xs):
    return [(x, pl.ANY) for x in xs]


def scalar(x):
    return [(x.reshape(-1).astype(jnp.int32), pltpu.SMEM)]


def plan(slab_count, group):
    full = slab_count // (2 * group)
    return [1] if full < 2 else [2] + [1] * (full - 1) + [2]


def after(xs, tokens, work=0):
    def body(ins, outs, scratch):
        yield

    outs = [(x.shape, x.dtype, pl.ANY) for x in xs]
    step = Step(body, outs, outside(xs), aliases={i: i for i in range(len(xs))}, work=work)
    return call([step], tokens)[0]


def first_transform(slabs, blocks, me, core, firsts, cuts, group, work=0):
    n = len(blocks)
    rows, cols = blocks[0].shape
    depth, width = slabs.shape[1:]
    amounts = [group if cut == 2 else 2 * group for cut in cuts]
    begins = [sum(amounts[:i]) for i in range(len(cuts))]

    def body(ins, outs, scratch):
        me_now, core_now, place, slab_hbm, *held = ins
        panel, buffer, sems = scratch
        copies = [
            [
                pltpu.make_async_copy(
                    slab_hbm.at[place[begins[i] + j]], buffer.at[i % 2, j], sems.at[i % 2, j]
                )
                for j in range(amount)
            ]
            for i, amount in enumerate(amounts)
        ]
        for batch in copies[:2]:
            for copy in batch:
                copy.start()
        yield
        for v in range(n):
            first = pl.multiple_of((me_now[0] ^ v) * rows, rows)
            panel[pl.ds(first, rows), :] = held[v][...]
        for i, amount in enumerate(amounts):
            for copy in copies[i]:
                copy.wait()
            result = jnp.dot(
                buffer[i % 2, :amount].reshape(amount * depth, width),
                panel[...],
                preferred_element_type=jnp.float32,
            )
            result = result.astype(jnp.bfloat16).reshape(amount, depth, cols)
            kept, other = outs[2 * i : 2 * i + 2]
            if cuts[i] == 1:
                kept[...], other[...] = result[:group], result[group:]
            else:
                low, high = result[:, :, : cols // 2], result[:, :, cols // 2 :]

                @pl.when(core_now[0] == 0)
                def _(kept=kept, other=other, low=low, high=high):
                    kept[...], other[...] = low, high

                @pl.when(core_now[0] == 1)
                def _(kept=kept, other=other, low=low, high=high):
                    kept[...], other[...] = high, low

            for batch in copies[i + 2 : i + 3]:
                for copy in batch:
                    copy.start()

    return Step(
        body,
        [
            ((group, depth, cols // cut), jnp.bfloat16, pltpu.VMEM)
            for cut in cuts
            for _ in range(2)
        ],
        scalar(me) + scalar(core) + scalar(firsts) + [(slabs, pltpu.HBM)] + inside(blocks),
        [
            pltpu.VMEM((n * rows, cols), jnp.bfloat16),
            pltpu.VMEM((2, max(amounts), depth, width), jnp.bfloat16),
            pltpu.SemaphoreType.DMA((2, max(amounts))),
        ],
        work=work,
    )


def merge_cores(kept, came):
    group, depth, cols = kept.shape

    def body(ins, outs, scratch):
        yield
        for j in range(group):
            outs[j][:depth, :] = ins[0][j]
            outs[j][depth:, :] = ins[1][j]

    return Step(
        body, [((2 * depth, cols), jnp.bfloat16, pltpu.VMEM)] * group, inside([kept, came])
    )


def pick_rows(chosen, blocks, work):
    rows, width = blocks[0].shape
    listed = chosen.shape[0]
    amount = len(blocks)

    def body(ins, outs, scratch):
        chosen_ref, *held = ins
        buffer, sems = scratch
        copies = []
        for i in range(amount):
            target = buffer.at[pl.ds(i * rows, rows)]
            copies.append(pltpu.make_async_copy(held[i], target, sems.at[i]))
            copies[i].start()
        yield
        for i in range(0, amount, 2):
            copies[i].wait()
            copies[i + 1].wait()
            result = lax.dot_general(
                chosen_ref[...],
                buffer[i * rows : (i + 2) * rows, :],
                (((1,), (1,)), ((), ())),
                preferred_element_type=jnp.float32,
            )
            outs[0][:, i * rows : (i + 2) * rows] = result.astype(jnp.bfloat16)

    return Step(
        body,
        [((listed, rows * amount), jnp.bfloat16, pltpu.VMEM)],
        inside([chosen]) + outside(blocks),
        [
            pltpu.VMEM((rows * amount, width), jnp.bfloat16),
            pltpu.SemaphoreType.DMA((amount,)),
        ],
        work=work,
    )


def second_transform(picked, parts, side, work):
    rows, cols = parts[0].shape
    share = picked.shape[0] // 2

    def body(ins, outs, scratch):
        side_now, picked_ref, *held = ins
        far, near = outs
        yield
        here = pl.ds(pl.multiple_of(side_now[0] * share, share), share)
        there = pl.ds(pl.multiple_of((1 - side_now[0]) * share, share), share)

        def total(lines):
            return sum(
                jnp.dot(
                    picked_ref[lines, j * rows : (j + 1) * rows],
                    x[...],
                    preferred_element_type=jnp.float32,
                )
                for j, x in enumerate(held)
            )

        far[...] = total(there).astype(jnp.bfloat16)
        near[...] = total(here)

    return Step(
        body,
        [
            ((share, cols), jnp.bfloat16, pltpu.VMEM),
            ((share, cols), jnp.float32, pltpu.VMEM),
        ],
        scalar(side) + inside([picked] + parts),
        work=work,
    )


def add_sides(near, came, member, group, work):
    rows, cols = near.shape
    share = rows // group

    def body(ins, outs, scratch):
        member_now, near_ref, came_ref = ins
        yield
        for j in range(group):
            lines = pl.ds(pl.multiple_of((member_now[0] ^ j) * share, share), share)
            total = near_ref[lines, :] + came_ref[lines, :].astype(jnp.float32)
            outs[j][...] = total.astype(jnp.bfloat16)

    return Step(
        body,
        [((share, cols), jnp.bfloat16, pltpu.VMEM)] * group,
        scalar(member) + inside([near, came]),
        work=work,
    )


def for_other_core(held, core):
    group = len(held)
    share, cols = held[0].shape[0] // 2, held[0].shape[1]

    def body(ins, outs, scratch):
        core_now, *refs = ins
        yield
        lines = pl.ds(pl.multiple_of((1 - core_now[0]) * share, share), share)
        for j, x in enumerate(refs):
            outs[0][j] = x[lines, :]

    return Step(
        body,
        [((group, share, cols), jnp.bfloat16, pltpu.VMEM)],
        scalar(core) + inside(held),
    )


def scale(slab_count, angular, held, came, order, core, cuts):
    share, cols = angular.shape
    group = len(held[0])
    batches = len(cuts)
    widths = [sum(cols // cut for cut in batch) for batch in cuts]
    amounts = [[group * (3 - cut) for cut in batch] for batch in cuts]
    chunks = sum(len(batch) for batch in cuts)

    def body(ins, outs, scratch):
        place, core_now, angular_ref, *refs = ins
        mine, theirs, sems, buffer, out_sems = scratch
        lines = pl.ds(pl.multiple_of(core_now[0] * share, share), share)
        copies = []
        for k in range(batches):
            wide = pl.ds(0, widths[k])
            pairs = [(refs[k * group + j].at[lines], mine.at[k, j, :, wide]) for j in range(group)]
            pairs.append((refs[batches * group + k], theirs.at[k, :, :, wide]))
            for source, target in pairs:
                copies.append(pltpu.make_async_copy(source, target, sems.at[len(copies)]))
                copies[-1].start()
        yield
        first, leaving = 0, []
        for k, batch in enumerate(cuts):
            for copy in copies[k * (group + 1) : (k + 1) * (group + 1)]:
                copy.wait()
            begin = 0
            for cut in batch:
                wide = slice(begin, begin + cols // cut)
                for kind in range(2):
                    source = core_now[0] if kind == 0 else 1 - core_now[0]
                    lanes = slice(None)
                    if cut == 2:
                        lanes = pl.ds(pl.multiple_of(source * (cols // 2), cols // 2), cols // 2)
                    factor = angular_ref[:, lanes]
                    for j in range(group):
                        slab = first + place[j] * (3 - cut) + (source if cut == 1 else 0)
                        x = (mine if kind == 0 else theirs)[k, j, :, wide]
                        value = factor * x.astype(jnp.float32)
                        buffer[slab, :, lanes] = value.astype(jnp.bfloat16)
                amount = group * (3 - cut)
                slabs_now = pl.ds(first, amount)
                copy = pltpu.make_async_copy(
                    buffer.at[slabs_now], outs[0].at[slabs_now], out_sems.at[len(leaving)]
                )
                copy.start()
                leaving.append(copy)
                first += amount
                begin += cols // cut
        yield
        for copy in leaving:
            copy.wait()

    flat = [x for xs in held for x in xs]
    return Step(
        body,
        [((slab_count, share, cols), jnp.bfloat16, pl.ANY)],
        scalar(order) + scalar(core) + inside([angular]) + outside(flat + came),
        [
            pltpu.VMEM((batches, group, share, max(widths)), jnp.bfloat16),
            pltpu.VMEM((batches, group, share, max(widths)), jnp.bfloat16),
            pltpu.SemaphoreType.DMA((batches * (group + 1),)),
            pltpu.VMEM((slab_count, share, cols), jnp.bfloat16),
            pltpu.SemaphoreType.DMA((chunks,)),
        ],
    )


def on_device(slabs, orbitals, channel_orbital, channel_target, coupling):
    n = lax.axis_size("blk")
    group = n // 4
    segment_now = lax.axis_index("segment")
    me = lax.axis_index("blk")
    core = me % 2
    member = (me // 2) % group
    side = me // (2 * group)
    channels = channel_orbital.shape[0]
    share = channels // n
    half_cols = channels // lax.axis_size("segment")
    slab_count = slabs.shape[0]
    splines = jnp.arange(orbitals.shape[1], dtype=jnp.int32)

    picks = lax.dynamic_slice_in_dim(channel_orbital, segment_now * half_cols, half_cols)
    onehot = (splines[:, None] == picks[None, :]).astype(jnp.bfloat16)
    mine = jnp.dot(orbitals, onehot, preferred_element_type=jnp.float32).astype(jnp.bfloat16)
    gathered = {0: mine}
    rows_of = {0: orbitals}
    bit = n // 2
    while bit:
        for v, x in list(gathered.items()):
            gathered[v ^ bit] = swap(x, bit)
        bit //= 2
    column_blocks = [gathered[v] for v in range(n)]

    kinds = jnp.arange(coupling.shape[0], dtype=jnp.int32)
    targets_rows = lax.dynamic_slice_in_dim(channel_target, me * share, share)
    targets_cols = lax.dynamic_slice_in_dim(channel_target, segment_now * half_cols, half_cols)
    onehot_rows = (targets_rows[:, None] == kinds[None, :]).astype(jnp.float32)
    onehot_cols = (kinds[:, None] == targets_cols[None, :]).astype(jnp.float32)
    angular = (
        jnp.dot(
            jnp.dot(
                onehot_rows, coupling.astype(jnp.float32), precision=lax.Precision.HIGHEST
            ),
            onehot_cols,
            precision=lax.Precision.HIGHEST,
        )
        / 16.0
    )

    order = member ^ jnp.arange(group, dtype=jnp.int32)
    cuts = plan(slab_count, group)
    last = len(cuts) - 1
    starts = [sum(group * (3 - cut) for cut in cuts[:k]) for k in range(last + 1)]
    kept, other, own, came, near, across, sums, held = {}, {}, {}, {}, {}, {}, {}, {}

    def transform(ks, tokens, work=0, trade=True):
        firsts = []
        for k in ks:
            if cuts[k] == 2:
                firsts.append(starts[k] + order)
            else:
                firsts += [starts[k] + 2 * order + core, starts[k] + 2 * order + 1 - core]
        step = first_transform(
            slabs,
            column_blocks,
            me,
            core,
            jnp.concatenate(firsts),
            [cuts[k] for k in ks],
            group,
            work,
        )
        flat = call([step], tokens, 36)[0]
        for i, k in enumerate(ks):
            kept[k], other[k] = flat[2 * i : 2 * i + 2]
            if trade:
                other[k] = swap(other[k], 1)

    def merge(ks, tokens):
        steps = [merge_cores(kept[k], other[k]) for k in ks]
        for k, result in zip(ks, call(steps, tokens), strict=True):
            own[k] = result

    def send(xs):
        return [swap(xs[j], 2 * j) for j in range(1, group)]

    transform([0], [angular])
    merge([0], [])
    came[0] = send(own[0])
    rows_of.update({2 * j: swap(orbitals, 2 * j) for j in range(1, group)})
    clock = after([jnp.zeros((8, 128), jnp.float32)], [own[0][0]], LONG)[0]
    if last:
        transform(list(range(1, last + 1)), [clock], 0, False)
        clock = kept[last]
    arrived = [v for v in rows_of if v]
    ready = after(
        came[0] + [rows_of[v] for v in arrived] + [other[k] for k in range(1, last + 1)], [clock]
    )
    came[0], ready = ready[: group - 1], ready[group - 1 :]
    rows_of.update(zip(arrived, ready, strict=False))
    for k in range(1, last + 1):
        other[k] = swap(ready[len(arrived) + k - 1], 1)
    token = came[0][0]
    if last:
        merge([1], [token])
        came[1] = send(own[1])
    for v, x in list(rows_of.items()):
        rows_of[v ^ 1] = swap(x, 1)

    chosen = (channel_orbital[:, None] == splines[None, :]).astype(jnp.bfloat16)
    rows = [rows_of[2 * j + c] for j in range(group) for c in range(2)]
    picked = call([pick_rows(chosen, rows, LONG)], [token])[0][0]

    token = picked
    for k in range(last + 1):
        work = MIDDLE if k else 0
        step = second_transform(picked, [own[k][0]] + came[k], side, work)
        far, near[k] = call([step], [token])[0]
        across[k] = swap(far, n // 2)
        token = far
        if k == 0 and last > 1:
            merge(list(range(2, last + 1)), [token])
        if 0 < k < last:
            came[k + 1] = send([None] + after(own[k + 1][1:], [before]))
        before = far
        if k:
            late = held[k - 2][1:] if k > 1 else []
            step = add_sides(near[k - 1], across[k - 1], member, group, MIDDLE)
            sums[k - 1] = call([step], [token] + late)[0]
            held[k - 1] = [sums[k - 1][0]] + send(sums[k - 1])
            token = sums[k - 1][0]
    clock = token
    final = {}
    for k in range(last):
        final[k] = swap(call([for_other_core(held[k], core)], [token])[0][0], 1)
    sums[last] = call([add_sides(near[last], across[last], member, group, 0)], [clock])[0]
    held[last] = [sums[last][0]] + send(sums[last])
    final[last] = swap(call([for_other_core(held[last], core)])[0][0], 1)
    ks = range(last + 1)
    step = scale(
        slab_count,
        angular,
        [held[k] for k in ks],
        [final[k] for k in ks],
        order,
        core,
        [[cut] for cut in cuts],
    )
    return call([step], (), 40)[0][0]


def solution(mesh):
    return jax.shard_map(
        on_device,
        mesh=mesh,
        in_specs=(P(None, "blk", None), P("blk", None), P(), P(), P()),
        out_specs=P(None, "blk", "segment"),
        check_vma=False,
    )
```

```python
import jax
import jax.numpy as jnp
from jax import lax
from jax.experimental import pallas as pl
from jax.experimental.pallas import tpu as pltpu
from jax.sharding import PartitionSpec as P

MIB = 1024 * 1024
MIDDLE = 3 * 10**9
LONG = 10**11


def swap(x, bits):
    n = lax.axis_size("blk")
    return lax.ppermute(x, "blk", [(i, i ^ bits) for i in range(n)])


class Step:
    def __init__(self, body, outs, ins, scratch=(), aliases=None, work=0):
        self.body, self.outs, self.ins, self.work = body, outs, ins, work
        self.scratch, self.aliases = list(scratch), aliases or {}


def call(steps, tokens=(), room=20):
    ins = [x for step in steps for x in step.ins]
    outs = [x for step in steps for x in step.outs]
    scratch = [x for step in steps for x in step.scratch]
    aliases, first_in, first_out = {}, 0, 0
    for step in steps:
        aliases.update({first_in + i: first_out + o for i, o in step.aliases.items()})
        first_in += len(step.ins)
        first_out += len(step.outs)

    def body(*refs):
        left = [list(refs[: len(ins)]), list(refs[len(ins) + len(tokens) :])]
        left = [left[0], left[1][: len(outs)], left[1][len(outs) :]]

        def take(which, amount):
            taken, left[which] = left[which][:amount], left[which][amount:]
            return taken

        running = [
            step.body(
                take(0, len(step.ins)), take(1, len(step.outs)), take(2, len(step.scratch))
            )
            for step in steps
        ]
        for _ in range(3):
            for each in running:
                next(each, None)

    results = pl.pallas_call(
        body,
        out_shape=[jax.ShapeDtypeStruct(shape, kind) for shape, kind, _ in outs],
        in_specs=[pl.BlockSpec(memory_space=space) for _, space in ins]
        + [pl.BlockSpec(memory_space=pl.ANY)] * len(tokens),
        out_specs=[pl.BlockSpec(memory_space=space) for _, _, space in outs],
        scratch_shapes=scratch,
        input_output_aliases=aliases,
        compiler_params=pltpu.CompilerParams(vmem_limit_bytes=room * MIB),
        cost_estimate=pl.CostEstimate(
            flops=sum(step.work for step in steps), bytes_accessed=0, transcendentals=0
        ),
    )(*[x for x, _ in ins], *tokens)
    results = list(results)
    split = []
    for step in steps:
        split.append(results[: len(step.outs)])
        results = results[len(step.outs) :]
    return split


def inside(xs):
    return [(x, pltpu.VMEM) for x in xs]


def outside(xs):
    return [(x, pl.ANY) for x in xs]


def scalar(x):
    return [(x.reshape(-1).astype(jnp.int32), pltpu.SMEM)]


def plan(slab_count, group):
    full = slab_count // (2 * group)
    return [1] if full < 2 else [2] + [1] * (full - 1) + [2]


def after(xs, tokens, work=0):
    def body(ins, outs, scratch):
        yield

    outs = [(x.shape, x.dtype, pl.ANY) for x in xs]
    step = Step(body, outs, outside(xs), aliases={i: i for i in range(len(xs))}, work=work)
    return call([step], tokens)[0]


def first_transform(slabs, blocks, me, core, firsts, cuts, group, work=0):
    n = len(blocks)
    rows, cols = blocks[0].shape
    depth, width = slabs.shape[1:]
    amounts = [group if cut == 2 else 2 * group for cut in cuts]
    begins = [sum(amounts[:i]) for i in range(len(cuts))]

    def body(ins, outs, scratch):
        me_now, core_now, place, slab_hbm, *held = ins
        panel, buffer, sems = scratch
        copies = [
            [
                pltpu.make_async_copy(
                    slab_hbm.at[place[begins[i] + j]], buffer.at[i % 2, j], sems.at[i % 2, j]
                )
                for j in range(amount)
            ]
            for i, amount in enumerate(amounts)
        ]
        for batch in copies[:2]:
            for copy in batch:
                copy.start()
        yield
        for v in range(n):
            first = pl.multiple_of((me_now[0] ^ v) * rows, rows)
            panel[pl.ds(first, rows), :] = held[v][...]
        for i, amount in enumerate(amounts):
            for copy in copies[i]:
                copy.wait()
            result = jnp.dot(
                buffer[i % 2, :amount].reshape(amount * depth, width),
                panel[...],
                preferred_element_type=jnp.float32,
            )
            result = result.astype(jnp.bfloat16).reshape(amount, depth, cols)
            kept, other = outs[2 * i : 2 * i + 2]
            if cuts[i] == 1:
                kept[...], other[...] = result[:group], result[group:]
            else:
                low, high = result[:, :, : cols // 2], result[:, :, cols // 2 :]

                @pl.when(core_now[0] == 0)
                def _(kept=kept, other=other, low=low, high=high):
                    kept[...], other[...] = low, high

                @pl.when(core_now[0] == 1)
                def _(kept=kept, other=other, low=low, high=high):
                    kept[...], other[...] = high, low

            for batch in copies[i + 2 : i + 3]:
                for copy in batch:
                    copy.start()

    return Step(
        body,
        [
            ((group, depth, cols // cut), jnp.bfloat16, pltpu.VMEM)
            for cut in cuts
            for _ in range(2)
        ],
        scalar(me) + scalar(core) + scalar(firsts) + [(slabs, pltpu.HBM)] + inside(blocks),
        [
            pltpu.VMEM((n * rows, cols), jnp.bfloat16),
            pltpu.VMEM((2, max(amounts), depth, width), jnp.bfloat16),
            pltpu.SemaphoreType.DMA((2, max(amounts))),
        ],
        work=work,
    )


def merge_cores(kept, came):
    group, depth, cols = kept.shape

    def body(ins, outs, scratch):
        yield
        for j in range(group):
            outs[j][:depth, :] = ins[0][j]
            outs[j][depth:, :] = ins[1][j]

    return Step(
        body, [((2 * depth, cols), jnp.bfloat16, pltpu.VMEM)] * group, inside([kept, came])
    )


def pick_rows(chosen, blocks, work):
    rows, width = blocks[0].shape
    listed = chosen.shape[0]
    amount = len(blocks)

    def body(ins, outs, scratch):
        chosen_ref, *held = ins
        buffer, sems = scratch
        copies = []
        for i in range(amount):
            target = buffer.at[pl.ds(i * rows, rows)]
            copies.append(pltpu.make_async_copy(held[i], target, sems.at[i]))
            copies[i].start()
        yield
        for i in range(0, amount, 2):
            copies[i].wait()
            copies[i + 1].wait()
            result = lax.dot_general(
                chosen_ref[...],
                buffer[i * rows : (i + 2) * rows, :],
                (((1,), (1,)), ((), ())),
                preferred_element_type=jnp.float32,
            )
            outs[0][:, i * rows : (i + 2) * rows] = result.astype(jnp.bfloat16)

    return Step(
        body,
        [((listed, rows * amount), jnp.bfloat16, pltpu.VMEM)],
        inside([chosen]) + outside(blocks),
        [
            pltpu.VMEM((rows * amount, width), jnp.bfloat16),
            pltpu.SemaphoreType.DMA((amount,)),
        ],
        work=work,
    )


def second_transform(picked, parts, side, work):
    rows, cols = parts[0].shape
    share = picked.shape[0] // 2

    def body(ins, outs, scratch):
        side_now, picked_ref, *held = ins
        far, near = outs
        yield
        here = pl.ds(pl.multiple_of(side_now[0] * share, share), share)
        there = pl.ds(pl.multiple_of((1 - side_now[0]) * share, share), share)

        def total(lines):
            return sum(
                jnp.dot(
                    picked_ref[lines, j * rows : (j + 1) * rows],
                    x[...],
                    preferred_element_type=jnp.float32,
                )
                for j, x in enumerate(held)
            )

        far[...] = total(there).astype(jnp.bfloat16)
        near[...] = total(here)

    return Step(
        body,
        [
            ((share, cols), jnp.bfloat16, pltpu.VMEM),
            ((share, cols), jnp.float32, pltpu.VMEM),
        ],
        scalar(side) + inside([picked] + parts),
        work=work,
    )


def add_sides(near, came, member, group, work):
    rows, cols = near.shape
    share = rows // group

    def body(ins, outs, scratch):
        member_now, near_ref, came_ref = ins
        yield
        for j in range(group):
            lines = pl.ds(pl.multiple_of((member_now[0] ^ j) * share, share), share)
            total = near_ref[lines, :] + came_ref[lines, :].astype(jnp.float32)
            outs[j][...] = total.astype(jnp.bfloat16)

    return Step(
        body,
        [((share, cols), jnp.bfloat16, pltpu.VMEM)] * group,
        scalar(member) + inside([near, came]),
        work=work,
    )


def for_other_core(held, core):
    group = len(held)
    share, cols = held[0].shape[0] // 2, held[0].shape[1]

    def body(ins, outs, scratch):
        core_now, *refs = ins
        yield
        lines = pl.ds(pl.multiple_of((1 - core_now[0]) * share, share), share)
        for j, x in enumerate(refs):
            outs[0][j] = x[lines, :]

    return Step(
        body,
        [((group, share, cols), jnp.bfloat16, pltpu.VMEM)],
        scalar(core) + inside(held),
    )


def scale(slab_count, angular, held, came, order, core, cuts):
    share, cols = angular.shape
    group = len(held[0])
    batches = len(cuts)
    widths = [sum(cols // cut for cut in batch) for batch in cuts]
    amounts = [[group * (3 - cut) for cut in batch] for batch in cuts]
    chunks = sum(len(batch) for batch in cuts)

    def body(ins, outs, scratch):
        place, core_now, angular_ref, *refs = ins
        mine, theirs, sems, buffer, out_sems = scratch
        lines = pl.ds(pl.multiple_of(core_now[0] * share, share), share)
        copies = []
        for k in range(batches):
            wide = pl.ds(0, widths[k])
            pairs = [(refs[k * group + j].at[lines], mine.at[k, j, :, wide]) for j in range(group)]
            pairs.append((refs[batches * group + k], theirs.at[k, :, :, wide]))
            for source, target in pairs:
                copies.append(pltpu.make_async_copy(source, target, sems.at[len(copies)]))
                copies[-1].start()
        yield
        first, leaving = 0, []
        for k, batch in enumerate(cuts):
            for copy in copies[k * (group + 1) : (k + 1) * (group + 1)]:
                copy.wait()
            begin = 0
            for cut in batch:
                wide = slice(begin, begin + cols // cut)
                for kind in range(2):
                    source = core_now[0] if kind == 0 else 1 - core_now[0]
                    lanes = slice(None)
                    if cut == 2:
                        lanes = pl.ds(pl.multiple_of(source * (cols // 2), cols // 2), cols // 2)
                    factor = angular_ref[:, lanes]
                    for j in range(group):
                        slab = first + place[j] * (3 - cut) + (source if cut == 1 else 0)
                        x = (mine if kind == 0 else theirs)[k, j, :, wide]
                        value = factor * x.astype(jnp.float32)
                        buffer[slab, :, lanes] = value.astype(jnp.bfloat16)
                amount = group * (3 - cut)
                slabs_now = pl.ds(first, amount)
                copy = pltpu.make_async_copy(
                    buffer.at[slabs_now], outs[0].at[slabs_now], out_sems.at[len(leaving)]
                )
                copy.start()
                leaving.append(copy)
                first += amount
                begin += cols // cut
        yield
        for copy in leaving:
            copy.wait()

    flat = [x for xs in held for x in xs]
    return Step(
        body,
        [((slab_count, share, cols), jnp.bfloat16, pl.ANY)],
        scalar(order) + scalar(core) + inside([angular]) + outside(flat + came),
        [
            pltpu.VMEM((batches, group, share, max(widths)), jnp.bfloat16),
            pltpu.VMEM((batches, group, share, max(widths)), jnp.bfloat16),
            pltpu.SemaphoreType.DMA((batches * (group + 1),)),
            pltpu.VMEM((slab_count, share, cols), jnp.bfloat16),
            pltpu.SemaphoreType.DMA((chunks,)),
        ],
    )


def on_device(slabs, orbitals, channel_orbital, channel_target, coupling):
    n = lax.axis_size("blk")
    group = n // 4
    segment_now = lax.axis_index("segment")
    me = lax.axis_index("blk")
    core = me % 2
    member = (me // 2) % group
    side = me // (2 * group)
    channels = channel_orbital.shape[0]
    share = channels // n
    half_cols = channels // lax.axis_size("segment")
    slab_count = slabs.shape[0]
    splines = jnp.arange(orbitals.shape[1], dtype=jnp.int32)

    picks = lax.dynamic_slice_in_dim(channel_orbital, segment_now * half_cols, half_cols)
    onehot = (splines[:, None] == picks[None, :]).astype(jnp.bfloat16)
    mine = jnp.dot(orbitals, onehot, preferred_element_type=jnp.float32).astype(jnp.bfloat16)
    gathered = {0: mine}
    rows_of = {0: orbitals}
    bit = n // 2
    while bit:
        for v, x in list(gathered.items()):
            gathered[v ^ bit] = swap(x, bit)
        bit //= 2
    column_blocks = [gathered[v] for v in range(n)]

    kinds = jnp.arange(coupling.shape[0], dtype=jnp.int32)
    targets_rows = lax.dynamic_slice_in_dim(channel_target, me * share, share)
    targets_cols = lax.dynamic_slice_in_dim(channel_target, segment_now * half_cols, half_cols)
    onehot_rows = (targets_rows[:, None] == kinds[None, :]).astype(jnp.float32)
    onehot_cols = (kinds[:, None] == targets_cols[None, :]).astype(jnp.float32)
    angular = (
        jnp.dot(
            jnp.dot(
                onehot_rows, coupling.astype(jnp.float32), precision=lax.Precision.HIGHEST
            ),
            onehot_cols,
            precision=lax.Precision.HIGHEST,
        )
        / 16.0
    )

    order = member ^ jnp.arange(group, dtype=jnp.int32)
    cuts = plan(slab_count, group)
    last = len(cuts) - 1
    starts = [sum(group * (3 - cut) for cut in cuts[:k]) for k in range(last + 1)]
    kept, other, own, came, near, across, sums, held = {}, {}, {}, {}, {}, {}, {}, {}

    def transform(ks, tokens, work=0, trade=True):
        firsts = []
        for k in ks:
            if cuts[k] == 2:
                firsts.append(starts[k] + order)
            else:
                firsts += [starts[k] + 2 * order + core, starts[k] + 2 * order + 1 - core]
        step = first_transform(
            slabs,
            column_blocks,
            me,
            core,
            jnp.concatenate(firsts),
            [cuts[k] for k in ks],
            group,
            work,
        )
        flat = call([step], tokens, 42)[0]
        for i, k in enumerate(ks):
            kept[k], other[k] = flat[2 * i : 2 * i + 2]
            if trade:
                other[k] = swap(other[k], 1)

    def merge(ks, tokens):
        steps = [merge_cores(kept[k], other[k]) for k in ks]
        for k, result in zip(ks, call(steps, tokens), strict=True):
            own[k] = result

    def send(xs):
        return [swap(xs[j], 2 * j) for j in range(1, group)]

    transform([0], [angular])
    merge([0], [])
    came[0] = send(own[0])
    rows_of.update({2 * j: swap(orbitals, 2 * j) for j in range(1, group)})
    clock = after([jnp.zeros((8, 128), jnp.float32)], [own[0][0]], LONG)[0]
    if last:
        transform(list(range(1, last + 1)), [clock], 0, False)
        clock = kept[last]
    arrived = [v for v in rows_of if v]
    ready = after(
        came[0] + [rows_of[v] for v in arrived] + [other[k] for k in range(1, last + 1)], [clock]
    )
    came[0], ready = ready[: group - 1], ready[group - 1 :]
    rows_of.update(zip(arrived, ready, strict=False))
    for k in range(1, last + 1):
        other[k] = swap(ready[len(arrived) + k - 1], 1)
    token = came[0][0]
    if last:
        merge([1], [token])
        came[1] = send(own[1])
    for v, x in list(rows_of.items()):
        rows_of[v ^ 1] = swap(x, 1)

    chosen = (channel_orbital[:, None] == splines[None, :]).astype(jnp.bfloat16)
    rows = [rows_of[2 * j + c] for j in range(group) for c in range(2)]
    picked = call([pick_rows(chosen, rows, LONG)], [token])[0][0]

    token = picked
    for k in range(last + 1):
        work = MIDDLE if k else 0
        step = second_transform(picked, [own[k][0]] + came[k], side, work)
        far, near[k] = call([step], [token])[0]
        across[k] = swap(far, n // 2)
        token = far
        if k == 0 and last > 1:
            merge(list(range(2, last + 1)), [token])
        if 0 < k < last:
            came[k + 1] = send([None] + after(own[k + 1][1:], [before]))
        before = far
        if k:
            late = held[k - 2][1:] if k > 1 else []
            step = add_sides(near[k - 1], across[k - 1], member, group, MIDDLE)
            sums[k - 1] = call([step], [token] + late)[0]
            held[k - 1] = [sums[k - 1][0]] + send(sums[k - 1])
            token = sums[k - 1][0]
    clock = token
    final = {}
    for k in range(last):
        final[k] = swap(call([for_other_core(held[k], core)], [token])[0][0], 1)
    sums[last] = call([add_sides(near[last], across[last], member, group, MIDDLE)], [clock])[0]
    held[last] = [sums[last][0]] + send(sums[last])
    final[last] = swap(call([for_other_core(held[last], core)])[0][0], 1)
    ks = range(last + 1)
    step = scale(
        slab_count,
        angular,
        [held[k] for k in ks],
        [final[k] for k in ks],
        order,
        core,
        [[cut] for cut in cuts],
    )
    return call([step], (), 40)[0][0]


def solution(mesh):
    return jax.shard_map(
        on_device,
        mesh=mesh,
        in_specs=(P(None, "blk", None), P("blk", None), P(), P(), P()),
        out_specs=P(None, "blk", "segment"),
        check_vma=False,
    )
```
